128 devices in a mesh: bx: 8 (over x_hi, y), by: 16 (over x_lo, z, core).
Axes of the slice: x: 4 (x_hi: 2, x_lo: 2; x = x_hi * 2 + x_lo), y: 4, z: 4, core: 2. Of those that a mesh axis runs over, the one named last changes fastest.
Arguments:
- right_sides: bfloat16 [8, 16, 16, 32, 256], P('bx', 'by'), may hold values from -6 to 6
- transform: bfloat16 [8, 16, 16, 256, 256], P('bx', 'by'), may hold values from -0.375 to 0.375
- inverse: bfloat16 [8, 16, 16, 128, 128], P('bx', 'by'), may hold values from -0.5 to 0.5
- fill_lower: bfloat16 [8, 16, 16, 16, 128, 128], P('bx', 'by'), may hold values from -0.25 to 0.25
- fill_upper: bfloat16 [8, 16, 16, 16, 128, 128], P('bx', 'by'), may hold values from -0.25 to 0.25
- parent_rows: bfloat16 [8, 16, 16, 1024, 128], P('bx', 'by'), may hold values from -0.1875 to 0.1875
- neighbours: int32 [8, 16, 16, 16], P('bx', 'by'), may hold values from 0 to 26, as said below
- counts: int32 [8, 16, 16], P('bx', 'by'), may hold values from 2 to 16, as said below
- child_slot: int32 [8, 16, 16], P('bx', 'by'), may hold values from 0 to 7, as said below
Outputs:
- solved: bfloat16 [8, 16, 16, 32, 256], P('bx', 'by')
The draws below stay inside these ranges and needn't reach their ends.
Inputs may be any that keep to these rules, and one draw needn't show every extreme that they name: `neighbours`: codes name existing boxes adjacent to the box (never itself) within the first counts slots, all different; the remaining slots hold 13. `counts`: some box of every draw uses all 16 slots. `child_slot`: the eight children of each parent hold eight different slots.
All inputs are finite; a program needn't handle non-finite values.
Results may differ from the reference program's by a relative error of at most 0.012.
Values may be sent and summed in bfloat16 or wider, within the bound.
No kernel may reach another device: no remote copies, remote signals or barrier semaphores. Data moves between devices by JAX's collectives and lax.ppermute only.
A program may use at most 64 MiB of HBM per device.

```python
import jax
import jax.numpy as jnp
from jax import lax

NPTS = 256
RANK = 128
NRHS = 32
MAXNB = 16
BZ = 16
NX = 8
NY = 16


def neighbour_table(key):
    inner = jax.random.fold_in(key, 71)
    offsets = jnp.concatenate([jnp.arange(13, dtype=jnp.int32), jnp.arange(14, 27, dtype=jnp.int32)])
    step_x = offsets // 9 - 1
    step_y = offsets // 3 % 3 - 1
    step_z = offsets % 3 - 1
    coord_x = jnp.arange(NX, dtype=jnp.int32)[:, None, None, None]
    coord_y = jnp.arange(NY, dtype=jnp.int32)[None, :, None, None]
    coord_z = jnp.arange(BZ, dtype=jnp.int32)[None, None, :, None]
    inside = (coord_x + step_x >= 0) & (coord_x + step_x < NX) & (coord_y + step_y >= 0) & (coord_y + step_y < NY) & (coord_z + step_z >= 0) & (coord_z + step_z < BZ)
    scores = jax.random.randint(inner, (NX, NY, BZ, 26), 0, 2 ** 20) * 32 + jnp.arange(26, dtype=jnp.int32)
    scores = jnp.where(inside, scores, scores + 2 ** 26)
    ranking = jnp.argsort(scores, axis=-1)
    chosen = jnp.take_along_axis(jnp.broadcast_to(offsets, (NX, NY, BZ, 26)), ranking, axis=-1)[..., :MAXNB]
    available = jnp.sum(inside.astype(jnp.int32), axis=-1)
    sparse = jax.random.randint(jax.random.fold_in(key, 72), (NX, NY, BZ), 2, MAXNB // 2 + 1)
    wanted = jnp.where(coord_x[..., 0] >= NX // 2, MAXNB, sparse)
    used = jnp.minimum(wanted, available)
    slot_no = jnp.arange(MAXNB, dtype=jnp.int32)
    offset_codes = jnp.where(slot_no < used[..., None], chosen, 13)
    return (offset_codes.astype(jnp.int32), used.astype(jnp.int32))


def draw_neighbours(key, part):
    return neighbour_table(key)[0]


def draw_counts(key, part):
    return neighbour_table(key)[1]


def draw_child_slot(key, part):
    key = jax.random.fold_in(key, 29)
    scores = jax.random.randint(key, (NX // 2, NY // 2, BZ // 2, 8), 0, 2 ** 20) * 8 + jnp.arange(8, dtype=jnp.int32)
    slot_ids = jnp.argsort(scores, axis=-1).astype(jnp.int32)
    slot_ids = slot_ids.reshape(NX // 2, NY // 2, BZ // 2, 2, 2, 2).transpose(0, 3, 1, 4, 2, 5)
    return slot_ids.reshape(NX, NY, BZ)


def block_levels(rng, extent, shards, least, top_value):
    level, own = 1.0, jax.random.fold_in(rng, 6)
    for axis_at, blocks in shards:
        steps = jnp.exp(jax.random.uniform(jax.random.fold_in(own, axis_at), (blocks,), jnp.float32, least / len(shards), top_value / len(shards)))
        level = level * jnp.repeat(steps, extent[axis_at] // blocks).reshape([-1 if axis == axis_at else 1 for axis in range(len(extent))])
    return level


def scatter_about(key, extent, scale, bound, cuts=(), held_as=jnp.bfloat16):
    drawn = jax.random.normal(key, extent, jnp.float32) * scale
    if len(cuts) > 0:
        drawn = block_levels(key, extent, cuts, -0.22, 0.18) * drawn
    return jnp.clip(drawn, min=-bound, max=bound).astype(held_as)


def setup_inputs(seed: int = 0) -> dict:
    arg_keys = jax.random.split(jax.random.key(seed), 10)
    return {
        "right_sides": scatter_about(arg_keys[0], (NX, NY, BZ, NRHS, NPTS), 1.0, 6.0, ((0, 8), (1, 16))),
        "transform": scatter_about(arg_keys[1], (NX, NY, BZ, NPTS, NPTS), NPTS ** -0.5, 0.375, ((0, 8), (1, 16))),
        "inverse": scatter_about(arg_keys[2], (NX, NY, BZ, RANK, RANK), RANK ** -0.5, 0.5, ((0, 8), (1, 16))),
        "fill_lower": scatter_about(arg_keys[3], (NX, NY, BZ, MAXNB, RANK, RANK), (4 * RANK) ** -0.5, 0.25, ((0, 8), (1, 16))),
        "fill_upper": scatter_about(arg_keys[4], (NX, NY, BZ, MAXNB, RANK, RANK), (4 * RANK) ** -0.5, 0.25, ((0, 8), (1, 16))),
        "parent_rows": scatter_about(arg_keys[5], (NX, NY, BZ, 8 * RANK, RANK), (8 * RANK) ** -0.5, 0.1875, ((0, 8), (1, 16))),
        "neighbours": draw_neighbours(jax.random.fold_in(arg_keys[9], 71), 0),
        "counts": draw_counts(jax.random.fold_in(arg_keys[9], 71), 0),
        "child_slot": draw_child_slot(jax.random.fold_in(arg_keys[9], 71), 0),
    }


def couple(field, fill_blocks, neighbours, counts):
    count_x, count_y, count_z = field.shape[0], field.shape[1], field.shape[2]
    padded = jnp.pad(field, ((1, 1), (1, 1), (1, 1), (0, 0), (0, 0)))
    flattened = padded.reshape((count_x + 2) * (count_y + 2) * (count_z + 2), field.shape[3], field.shape[4])
    coord_x = jnp.arange(count_x, dtype=jnp.int32)[:, None, None]
    coord_y = jnp.arange(count_y, dtype=jnp.int32)[None, :, None]
    coord_z = jnp.arange(count_z, dtype=jnp.int32)[None, None, :]
    running = jnp.zeros(field.shape, jnp.float32)
    for slot_no in range(MAXNB):
        offset_codes = neighbours[:, :, :, slot_no]
        step_x = offset_codes // 9
        step_y = (offset_codes // 3) % 3
        step_z = offset_codes % 3
        positions = ((coord_x + step_x) * (count_y + 2) + coord_y + step_y) * (count_z + 2) + coord_z + step_z
        gathered = jnp.take(flattened, positions.reshape(-1).astype(jnp.int32), axis=0).reshape(field.shape)
        weights = fill_blocks[:, :, :, slot_no]
        product = jnp.einsum('abzrc,abzcd->abzrd', gathered.astype(jnp.float32), weights.astype(jnp.float32))
        active = (slot_no < counts)[:, :, :, None, None]
        running = running + jnp.where(active, product, jnp.zeros_like(product))
    return running


def slab_product(operands):
    left_side, right_side = operands
    return jnp.einsum('bzrk,bzkd->bzrd', left_side.astype(jnp.float32), right_side.astype(jnp.float32))


def reference(right_sides, transform, inverse, fill_lower, fill_upper, parent_rows, neighbours, counts, child_slot):
    count_x, count_y, count_z = right_sides.shape[0], right_sides.shape[1], right_sides.shape[2]
    projected = lax.map(slab_product, (right_sides, transform))
    redundant = projected[..., :RANK].astype(jnp.bfloat16)
    local_sol = lax.map(slab_product, (redundant, inverse)).astype(jnp.bfloat16)
    coupled = couple(local_sol, fill_lower, neighbours, counts)
    reduced = (projected[..., RANK:] - coupled).astype(jnp.bfloat16)
    half_x, half_y, half_z = count_x // 2, count_y // 2, count_z // 2
    children = reduced.reshape(half_x, 2, half_y, 2, half_z, 2, NRHS, RANK)
    children = children.transpose(0, 2, 4, 1, 3, 5, 6, 7).reshape(half_x, half_y, half_z, 8, NRHS, RANK)
    slot_ids = child_slot.reshape(half_x, 2, half_y, 2, half_z, 2).transpose(0, 2, 4, 1, 3, 5).reshape(half_x, half_y, half_z, 8)
    ordinal = jnp.arange(8, dtype=jnp.int32)
    onehot = (slot_ids[:, :, :, None, :] == ordinal[:, None]).astype(jnp.float32)
    stacked = jnp.einsum('abcjk,abckrd->abcrjd', onehot, children.astype(jnp.float32))
    stacked = stacked.reshape(half_x, half_y, half_z, NRHS, 8 * RANK).astype(jnp.bfloat16)
    spread = jnp.broadcast_to(stacked[:, None, :, None, :, None], (half_x, 2, half_y, 2, half_z, 2, NRHS, 8 * RANK))
    spread = spread.reshape(count_x, count_y, count_z, NRHS, 8 * RANK)
    skel_sol = lax.map(slab_product, (spread, parent_rows)).astype(jnp.bfloat16)
    backward = couple(skel_sol, fill_upper, neighbours, counts)
    red_sol = (local_sol.astype(jnp.float32) - backward).astype(jnp.bfloat16)
    whole = jnp.concatenate([red_sol, skel_sol], axis=-1)
    transposed = jnp.swapaxes(transform, 3, 4)
    solved = lax.map(slab_product, (whole, transposed))
    return solved.astype(jnp.bfloat16)
```

```python
import jax
import jax.numpy as jnp
from jax import lax
from jax.experimental import pallas as pl
from jax.experimental.pallas import tpu as pltpu
from jax.sharding import PartitionSpec as P

BF = jnp.bfloat16
F32 = jnp.float32
VM = pl.BlockSpec(memory_space=pltpu.VMEM)
SM = pl.BlockSpec(memory_space=pltpu.SMEM)


def resident(value):
    return pltpu.with_memory_space_constraint(value, pltpu.VMEM)


def even_pairs(peers):
    return [(i, i ^ 1) for i in range(peers)]


def odd_pairs(peers):
    return [(i, ((i + 1) ^ 1) - 1) for i in range(1, peers - 1)] + [(0, peers - 1), (peers - 1, 0)]


def even_swap(value, axis):
    return lax.ppermute(value, axis, even_pairs(lax.axis_size(axis)))


def odd_swap(value, axis):
    return lax.ppermute(value, axis, odd_pairs(lax.axis_size(axis)))


def first_kernel(rhs_ref, transform_ref, inverse_ref, slots_ref, skel_ref, field_ref):
    step = pl.program_id(0)
    block, rank = rhs_ref.shape[0], inverse_ref.shape[1]
    height = field_ref.shape[0] - 1

    @pl.when(step == 0)
    def _():
        rows = lax.broadcasted_iota(jnp.int32, (height, height), 0)
        cols = lax.broadcasted_iota(jnp.int32, (height, height), 1)
        column = jnp.sum(jnp.where(rows == cols, slots_ref[...], 0), axis=1, keepdims=True)
        plane = jnp.broadcast_to(column, (height, rank)).astype(F32)
        plane = jnp.concatenate([plane, jnp.zeros((field_ref.shape[1] - height, rank), F32)], axis=0)
        field_ref[height] = plane.astype(BF)

    for i in range(block):
        projected = jnp.dot(rhs_ref[i], transform_ref[i], preferred_element_type=F32)
        skel_ref[i] = projected[:, rank:]
        local = jnp.dot(projected[:, :rank].astype(BF), inverse_ref[i], preferred_element_type=F32)
        field_ref[step * block + i] = local.astype(BF)


def first(right_sides, transform, inverse, slots):
    height, rhs_count, points = right_sides.shape
    rank = inverse.shape[1]
    block = 4
    return pl.pallas_call(
        first_kernel,
        grid=(height // block,),
        in_specs=[
            pl.BlockSpec((block, rhs_count, points), lambda i: (i, 0, 0)),
            pl.BlockSpec((block, points, points), lambda i: (i, 0, 0)),
            pl.BlockSpec((block, rank, rank), lambda i: (i, 0, 0)),
            pl.BlockSpec((1, height), lambda i: (0, 0)),
        ],
        out_specs=[
            pl.BlockSpec((block, rhs_count, rank), lambda i: (i, 0, 0)),
            pl.BlockSpec((height + 1, rhs_count, rank), lambda i: (0, 0, 0)),
        ],
        out_shape=[
            jax.ShapeDtypeStruct((height, rhs_count, rank), F32),
            jax.ShapeDtypeStruct((height + 1, rhs_count, rank), BF),
        ],
        compiler_params=pltpu.CompilerParams(vmem_limit_bytes=8 << 20),
        name="first",
    )(right_sides, transform, inverse, slots)


def fill_table(table_ref, parts):
    planes = parts[0].shape[0]
    for i, part in enumerate(parts):
        table_ref[i * planes : (i + 1) * planes] = part[...]
    table_ref[len(parts) * planes] = jnp.zeros(table_ref.shape[1:], BF)


def coupling(table_ref, where_ref, fill_ref, z):
    slots, rank = fill_ref.shape[1], fill_ref.shape[2]
    rows = jnp.concatenate([table_ref[where_ref[z, k]] for k in range(slots)], axis=1)
    blocks = fill_ref[z].reshape(slots * rank, fill_ref.shape[3])
    return jnp.dot(rows, blocks, preferred_element_type=F32)


def lower_kernel(where_ref, own_ref, even_ref, odd_ref, skel_ref, fill_ref, out_ref, table_ref):
    fill_table(table_ref, (own_ref, even_ref, odd_ref))

    def box(z, _):
        out_ref[z] = (skel_ref[z] - coupling(table_ref, where_ref, fill_ref, z)).astype(BF)
        return _

    lax.fori_loop(0, out_ref.shape[0], box, 0, unroll=2)


def lower(where, own, even, odd, skel, fill):
    height, rhs_count, rank = skel.shape
    return pl.pallas_call(
        lower_kernel,
        in_specs=[SM, VM, VM, VM, VM, VM],
        out_specs=VM,
        out_shape=jax.ShapeDtypeStruct((height, rhs_count, rank), BF),
        scratch_shapes=[pltpu.VMEM((3 * own.shape[0] + 1, rhs_count, rank), BF)],
        compiler_params=pltpu.CompilerParams(vmem_limit_bytes=8 << 20),
        name="lower",
    )(where, resident(own), resident(even), resident(odd), resident(skel), resident(fill))


def parent_kernel(where_ref, own_ref, far_ref, rows_ref, out_ref, table_ref):
    planes = own_ref.shape[0]
    table_ref[0:planes] = own_ref[...]
    table_ref[planes : 2 * planes] = far_ref[...]

    def parent(i, _):
        stacked = jnp.concatenate([table_ref[where_ref[i, s]] for s in range(8)], axis=1)
        for e in range(2):
            z = 2 * i + e
            out_ref[z] = jnp.dot(stacked, rows_ref[z], preferred_element_type=F32).astype(BF)
        return _

    lax.fori_loop(0, out_ref.shape[0] // 2, parent, 0, unroll=2)


def parent(where, own, far, rows):
    height, rhs_count, rank = rows.shape[0], own.shape[1], own.shape[2]
    return pl.pallas_call(
        parent_kernel,
        in_specs=[SM, VM, VM, VM],
        out_specs=VM,
        out_shape=jax.ShapeDtypeStruct((height, rhs_count, rank), BF),
        scratch_shapes=[pltpu.VMEM((2 * own.shape[0], rhs_count, rank), BF)],
        compiler_params=pltpu.CompilerParams(vmem_limit_bytes=8 << 20),
        name="parent",
    )(where, resident(own), resident(far), resident(rows))


def upper_kernel(where_ref, own_ref, even_ref, odd_ref, skel_ref, local_ref, fill_ref, transform_ref, out_ref, table_ref):
    fill_table(table_ref, (own_ref, even_ref, odd_ref))
    last = (((1,), (1,)), ((), ()))

    def box(z, _):
        backward = coupling(table_ref, where_ref, fill_ref, z)
        red = (local_ref[z].astype(F32) - backward).astype(BF)
        whole = jnp.concatenate([red, skel_ref[z]], axis=1)
        solved = lax.dot_general(whole, transform_ref[z], last, preferred_element_type=F32)
        out_ref[z] = solved.astype(BF)
        return _

    lax.fori_loop(0, out_ref.shape[0], box, 0, unroll=2)


def upper(where, own, even, odd, skel, local, fill, transform):
    height, rhs_count, rank = skel.shape
    points = transform.shape[1]
    return pl.pallas_call(
        upper_kernel,
        in_specs=[SM, VM, VM, VM, VM, VM, VM, VM],
        out_specs=VM,
        out_shape=jax.ShapeDtypeStruct((height, rhs_count, points), BF),
        scratch_shapes=[pltpu.VMEM((3 * own.shape[0] + 1, rhs_count, rank), BF)],
        compiler_params=pltpu.CompilerParams(vmem_limit_bytes=8 << 20),
        name="upper",
    )(
        where,
        resident(own),
        resident(even),
        resident(odd),
        resident(skel),
        resident(local),
        resident(fill),
        resident(transform),
    )


def halo(field):
    even = even_swap(field, "bx")
    odd = odd_swap(field, "bx")
    own = jnp.concatenate([field, even, odd], axis=0)
    return own, even_swap(own, "by"), odd_swap(own, "by")


def places(neighbours, counts, planes):
    height, slots = neighbours.shape
    step_x = neighbours // 9 - 1
    step_y = neighbours // 3 % 3 - 1
    step_z = neighbours % 3 - 1

    def source(step, axis):
        toward_even = 1 - 2 * (lax.axis_index(axis) % 2)
        return jnp.where(step == 0, 0, jnp.where(step == toward_even, 1, 2))

    column = source(step_y, "by") * 3 + source(step_x, "bx")
    height_at = jnp.arange(height, dtype=jnp.int32)[:, None] + step_z
    active = jnp.arange(slots, dtype=jnp.int32)[None, :] < counts[:, None]
    return jnp.where(active, column * planes + height_at, 9 * planes)


def body(right_sides, transform, inverse, fill_lower, fill_upper, parent_rows, neighbours, counts, child_slot):
    right_sides, transform, inverse = right_sides[0, 0], transform[0, 0], inverse[0, 0]
    height = right_sides.shape[0]
    skel, field = first(right_sides, transform, inverse, child_slot[0])
    planes = height + 1
    own, even, odd = halo(field)
    slots = jnp.stack([own[height, :height, 0], own[planes + height, :height, 0], even[height, :height, 0], even[planes + height, :height, 0]])
    slots = slots.astype(jnp.int32).reshape(4, height // 2, 2)
    ordinal = jnp.arange(8, dtype=jnp.int32)
    index = jnp.arange(4 * height, dtype=jnp.int32).reshape(4, height // 2, 2)
    hit = slots[..., None] == ordinal
    where_child = jnp.sum(jnp.where(hit, index[..., None], 0), axis=(0, 2))
    where = places(neighbours[0, 0], counts[0, 0], planes)
    reduced = lower(where, own, even, odd, skel, fill_lower[0, 0])
    pair = jnp.concatenate([reduced, even_swap(reduced, "bx")], axis=0)
    skel_sol = parent(where_child, pair, even_swap(pair, "by"), parent_rows[0, 0])
    where = jnp.where(where == 9 * planes, 9 * height, where - where // planes)
    own, even, odd = halo(skel_sol)
    solved = upper(where, own, even, odd, skel_sol, field, fill_upper[0, 0], transform)
    return solved[None, None]


def solution(mesh):
    wide = P("bx", "by", None, None, None)
    placed = (wide, wide, wide, P("bx", "by", None, None, None, None), P("bx", "by", None, None, None, None), wide)
    placed = placed + (P("bx", "by", None, None), P("bx", "by", None), P("bx", "by", None))
    return jax.shard_map(body, mesh=mesh, in_specs=placed, out_specs=wide, check_vma=False)
```

```python
import functools

import jax
import jax.numpy as jnp
from jax import lax
from jax.experimental import pallas as pl
from jax.experimental.pallas import tpu as pltpu
from jax.sharding import PartitionSpec as P

BF = jnp.bfloat16
F32 = jnp.float32
VM = pl.BlockSpec(memory_space=pltpu.VMEM)
SM = pl.BlockSpec(memory_space=pltpu.SMEM)
HB = pl.BlockSpec(memory_space=pltpu.HBM)
AN = pl.BlockSpec(memory_space=pl.ANY)


def resident(value):
    return pltpu.with_memory_space_constraint(value, pltpu.VMEM)


def far_memory(value):
    return pltpu.with_memory_space_constraint(value, pltpu.HBM)


def scalars(value):
    return pltpu.with_memory_space_constraint(value, pltpu.SMEM)


def call(kernel, name, ins, outs, scratch=(), moved=0, flops=0):
    return pl.pallas_call(
        kernel,
        in_specs=ins,
        out_specs=[SM if getattr(o, "memory_space", None) == pltpu.SMEM else VM for o in outs],
        out_shape=list(outs),
        scratch_shapes=list(scratch),
        compiler_params=pltpu.CompilerParams(vmem_limit_bytes=4 << 20),
        cost_estimate=pl.CostEstimate(flops=flops, bytes_accessed=moved, transcendentals=0),
        name=name,
    )


def even_pairs(peers):
    return [(i, i ^ 1) for i in range(peers)]


def odd_pairs(peers):
    return [(i, ((i + 1) ^ 1) - 1) for i in range(1, peers - 1)] + [(0, peers - 1), (peers - 1, 0)]


def even_swap(value, axis):
    return lax.ppermute(value, axis, even_pairs(lax.axis_size(axis)))


def odd_swap(value, axis):
    return lax.ppermute(value, axis, odd_pairs(lax.axis_size(axis)))


def first_kernel(rhs_hbm, transform_hbm, inverse_hbm, slots_hbm, skel_ref, field_ref, transform_ref, rhs_ref, inverse_ref, slots_ref, sems):
    height, rank = inverse_ref.shape[0], inverse_ref.shape[1]
    bounds = (0, height * 3 // 8, height * 3 // 4, height)
    chunks = [slice(i, j) for i, j in zip(bounds[:-1], bounds[1:])]
    loads = [pltpu.make_async_copy(transform_hbm.at[c], transform_ref.at[c], sems.at[i]) for i, c in enumerate(chunks)]
    rhs_load = pltpu.make_async_copy(rhs_hbm, rhs_ref, sems.at[3])
    inverse_load = pltpu.make_async_copy(inverse_hbm, inverse_ref, sems.at[4])
    small = pltpu.make_async_copy(slots_hbm, slots_ref, sems.at[5])
    for copy in (rhs_load, *loads, inverse_load, small):
        copy.start()
    rhs_load.wait()
    redundant = []
    for c, load in zip(chunks, loads):
        load.wait()
        boxes = range(c.start, c.stop)
        projected = [jnp.dot(rhs_ref[z], transform_ref[z], preferred_element_type=F32) for z in boxes]
        for z, rows in zip(boxes, projected):
            skel_ref[z] = rows[:, rank:]
            redundant.append(rows[:, :rank].astype(BF))
    inverse_load.wait()
    for z in range(height):
        field_ref[z] = jnp.dot(redundant[z], inverse_ref[z], preferred_element_type=F32).astype(BF)
    small.wait()
    rows = lax.broadcasted_iota(jnp.int32, (height, height), 0)
    cols = lax.broadcasted_iota(jnp.int32, (height, height), 1)
    column = jnp.sum(jnp.where(rows == cols, slots_ref[...], 0), axis=1, keepdims=True)
    plane = jnp.broadcast_to(column, (height, rank)).astype(F32)
    plane = jnp.concatenate([plane, jnp.zeros((field_ref.shape[1] - height, rank), F32)], axis=0)
    field_ref[height] = plane.astype(BF)


def first(right_sides, transform, inverse, slots):
    height, rhs_count, points = right_sides.shape
    rank = inverse.shape[1]
    return call(
        first_kernel,
        "first",
        [HB, HB, HB, HB],
        [
            pltpu.VMEM((height, rhs_count, rank), F32),
            pltpu.VMEM((height + 1, rhs_count, rank), BF),
            pltpu.VMEM(transform.shape, BF),
        ],
        [
            pltpu.VMEM(right_sides.shape, BF),
            pltpu.VMEM(inverse.shape, BF),
            pltpu.VMEM(slots.shape, jnp.int32),
            pltpu.SemaphoreType.DMA((6,)),
        ],
    )(far_memory(right_sides), far_memory(transform), far_memory(inverse), far_memory(slots))


def fetch_kernel(value_hbm, after_ref, out_ref, token_ref, sem):
    copy = pltpu.make_async_copy(value_hbm, out_ref, sem)
    copy.start()
    token_ref[...] = jnp.zeros_like(token_ref)
    copy.wait()


def fetch(value, after):
    return call(
        fetch_kernel,
        "fetch",
        [HB, AN],
        [pltpu.VMEM(value.shape, value.dtype), pltpu.VMEM((8, 128), F32)],
        [pltpu.SemaphoreType.DMA],
        moved=2 * value.size * value.dtype.itemsize,
    )(far_memory(value), after)


def places_kernel(lists_hbm, counts_hbm, after_ref, out_ref, lists_ref, counts_ref, found_ref, sems, *, planes):
    height, slots = lists_ref.shape
    loads = [pltpu.make_async_copy(lists_hbm, lists_ref, sems.at[0]), pltpu.make_async_copy(counts_hbm, counts_ref, sems.at[1])]
    for load in loads:
        load.start()
    for load in loads:
        load.wait()
    codes = lists_ref[...]
    one = jnp.int32(1)
    step_x = jnp.where(codes >= 9, one, 0) + jnp.where(codes >= 18, one, 0)
    rest = codes - 9 * step_x
    step_y = jnp.where(rest >= 3, one, 0) + jnp.where(rest >= 6, one, 0)
    step_z = rest - 3 * step_y

    def source(step, axis):
        even_side = 2 - 2 * (lax.axis_index(axis) % 2)
        return jnp.where(step == 1, 0, jnp.where(step == even_side, one, 2))

    level = lax.broadcasted_iota(jnp.int32, (height, height), 0)
    lane = lax.broadcasted_iota(jnp.int32, (height, height), 1)
    counts = jnp.sum(jnp.where(level == lane, counts_ref[...], 0), axis=1, keepdims=True)
    active = lax.broadcasted_iota(jnp.int32, (height, slots), 1) < counts
    column = source(step_y, "by") * 3 + source(step_x, "bx")
    level = lax.broadcasted_iota(jnp.int32, (height, slots), 0) + step_z - 1
    for i, size in enumerate(planes):
        found_ref[i * height : (i + 1) * height] = jnp.where(active, column * size + level, 9 * size)
    copy = pltpu.make_async_copy(found_ref, out_ref, sems.at[2])
    copy.start()
    copy.wait()


def places(neighbours, counts, planes, after):
    height, slots = neighbours.shape
    rows = len(planes) * height
    return call(
        functools.partial(places_kernel, planes=planes),
        "places",
        [HB, HB, AN],
        [pltpu.SMEM((rows, slots), jnp.int32)],
        [
            pltpu.VMEM(neighbours.shape, jnp.int32),
            pltpu.VMEM(counts.shape, jnp.int32),
            pltpu.VMEM((rows, slots), jnp.int32),
            pltpu.SemaphoreType.DMA((3,)),
        ],
        moved=1 << 20,
    )(far_memory(neighbours), far_memory(counts), after)[0]


def pack_kernel(*refs):
    out_ref = refs[-1]
    planes = refs[0].shape[0]
    for i in range(out_ref.shape[0] // planes):
        out_ref[i * planes : (i + 1) * planes] = refs[i][...]


def pack(parts, after):
    planes, rows, cols = parts[0].shape
    shape = pltpu.VMEM((len(parts) * planes, rows, cols), BF)
    return call(pack_kernel, "pack", [VM] * len(parts) + [AN] * len(after), [shape])(*map(resident, parts), *after)[0]


def fill_table(table_ref, parts):
    planes = parts[0].shape[0]
    for i, part in enumerate(parts):
        table_ref[i * planes : (i + 1) * planes] = part[...]
    table_ref[len(parts) * planes] = jnp.zeros(table_ref.shape[1:], BF)


def coupling(table_ref, where_ref, base, fill_ref, z):
    slots, rank = fill_ref.shape[1], fill_ref.shape[2]
    rows = jnp.concatenate([table_ref[where_ref[base + z, k]] for k in range(slots)], axis=1)
    blocks = fill_ref[z].reshape(slots * rank, fill_ref.shape[3])
    return jnp.dot(rows, blocks, preferred_element_type=F32)


def lower_kernel(where_ref, own_ref, even_ref, odd_ref, skel_ref, fill_ref, after_ref, out_ref, child_ref, table_ref, child_vmem, sem):
    height, planes = out_ref.shape[0], own_ref.shape[0] // 3
    lane = lax.broadcasted_iota(jnp.int32, child_vmem.shape, 1)
    level = lax.broadcasted_iota(jnp.int32, child_vmem.shape, 0)
    found = jnp.zeros(child_vmem.shape, jnp.int32)
    columns = (own_ref[height], own_ref[planes + height], even_ref[height], even_ref[planes + height])
    for i, column in enumerate(columns):
        slots = column.astype(F32)[:height].astype(jnp.int32)
        found = found + jnp.where(slots == lane, i * height + level, 0)
    child_vmem[...] = found
    copy = pltpu.make_async_copy(child_vmem, child_ref, sem)
    copy.start()
    fill_table(table_ref, (own_ref, even_ref, odd_ref))
    for z in range(height):
        out_ref[z] = (skel_ref[z] - coupling(table_ref, where_ref, 0, fill_ref, z)).astype(BF)
    copy.wait()


def lower(where, own, even, odd, skel, fill, after):
    height, rhs_count, rank = skel.shape
    return call(
        lower_kernel,
        "lower",
        [SM, VM, VM, VM, VM, VM, AN],
        [pltpu.VMEM((height, rhs_count, rank), BF), pltpu.SMEM((height, rank), jnp.int32)],
        [
            pltpu.VMEM((3 * own.shape[0] + 1, rhs_count, rank), BF),
            pltpu.VMEM((height, rank), jnp.int32),
            pltpu.SemaphoreType.DMA,
        ],
    )(scalars(where), resident(own), resident(even), resident(odd), resident(skel), resident(fill), after)


def parent_kernel(child_ref, own_ref, far_ref, rows_ref, out_ref, table_ref):
    planes = own_ref.shape[0]
    table_ref[0:planes] = own_ref[...]
    table_ref[planes : 2 * planes] = far_ref[...]
    for i in range(out_ref.shape[0] // 2):
        places = [child_ref[2 * i, s] + child_ref[2 * i + 1, s] for s in range(8)]
        stacked = jnp.concatenate([table_ref[place] for place in places], axis=1)
        for z in (2 * i, 2 * i + 1):
            out_ref[z] = jnp.dot(stacked, rows_ref[z], preferred_element_type=F32).astype(BF)


def parent(child, own, far, rows):
    height, rhs_count, rank = rows.shape[0], own.shape[1], own.shape[2]
    return call(
        parent_kernel,
        "parent",
        [SM, VM, VM, VM],
        [pltpu.VMEM((height, rhs_count, rank), BF)],
        [pltpu.VMEM((2 * own.shape[0], rhs_count, rank), BF)],
    )(scalars(child), resident(own), resident(far), resident(rows))[0]


def upper_kernel(where_ref, own_ref, even_ref, odd_ref, skel_ref, local_ref, fill_ref, transform_ref, out_ref, table_ref):
    fill_table(table_ref, (own_ref, even_ref, odd_ref))
    last = (((1,), (1,)), ((), ()))
    height = out_ref.shape[0]
    for z in range(height):
        backward = coupling(table_ref, where_ref, height, fill_ref, z)
        red = (local_ref[z].astype(F32) - backward).astype(BF)
        whole = jnp.concatenate([red, skel_ref[z]], axis=1)
        solved = lax.dot_general(whole, transform_ref[z], last, preferred_element_type=F32)
        out_ref[z] = solved.astype(BF)


def upper(where, own, even, odd, skel, local, fill, transform):
    height, rhs_count, rank = skel.shape
    points = transform.shape[1]
    operands = (own, even, odd, skel, local, fill, transform)
    return call(
        upper_kernel,
        "upper",
        [SM, VM, VM, VM, VM, VM, VM, VM],
        [jax.ShapeDtypeStruct((height, rhs_count, points), BF)],
        [pltpu.VMEM((3 * own.shape[0] + 1, rhs_count, rank), BF)],
    )(scalars(where), *map(resident, operands))[0]


def halo(field, after):
    odd = odd_swap(field, "bx")
    even = even_swap(field, "bx")
    own = pack([field, even, odd], after)
    return own, even_swap(own, "by"), odd_swap(own, "by")


def body(right_sides, transform, inverse, fill_lower, fill_upper, parent_rows, neighbours, counts, child_slot):
    right_sides, transform, inverse = right_sides[0, 0], transform[0, 0], inverse[0, 0]
    height = right_sides.shape[0]
    skel, field, transform = first(right_sides, transform, inverse, child_slot[0])
    planes = height + 1
    fill_lower, token = fetch(fill_lower[0, 0], field)
    own, even, odd = halo(field, [token])
    where = places(neighbours[0, 0], counts[0], (planes, height), own)
    parent_rows, token = fetch(parent_rows[0, 0], own)
    reduced, child = lower(where, own, even, odd, skel, fill_lower, token)
    fill_upper, token = fetch(fill_upper[0, 0], reduced)
    pair = pack([reduced, even_swap(reduced, "bx")], [token])
    skel_sol = parent(child, pair, even_swap(pair, "by"), parent_rows)
    own, even, odd = halo(skel_sol, [])
    solved = upper(where, own, even, odd, skel_sol, field, fill_upper, transform)
    return solved[None, None]


def solution(mesh):
    wide = P("bx", "by", None, None, None)
    placed = (wide, wide, wide, P("bx", "by", None, None, None, None), P("bx", "by", None, None, None, None), wide)
    placed = placed + (P("bx", "by", None, None), P("bx", "by", None), P("bx", "by", None))
    return jax.shard_map(body, mesh=mesh, in_specs=placed, out_specs=wide, check_vma=False)
```

```python
import functools
import math

import jax
import jax.numpy as jnp
from jax import lax
from jax.experimental import pallas as pl
from jax.experimental.pallas import tpu as pltpu
from jax.sharding import PartitionSpec as P

BF = jnp.bfloat16
F32 = jnp.float32
VM = pl.BlockSpec(memory_space=pltpu.VMEM)
SM = pl.BlockSpec(memory_space=pltpu.SMEM)
HB = pl.BlockSpec(memory_space=pltpu.HBM)
AN = pl.BlockSpec(memory_space=pl.ANY)
TOKEN = pltpu.VMEM((8, 128), F32)


def resident(value):
    return pltpu.with_memory_space_constraint(value, pltpu.VMEM)


def far_memory(value):
    return pltpu.with_memory_space_constraint(value, pltpu.HBM)


def scalars(value):
    return pltpu.with_memory_space_constraint(value, pltpu.SMEM)


def call(kernel, name, ins, outs, scratch=(), moved=0, flops=0):
    return pl.pallas_call(
        kernel,
        in_specs=ins,
        out_specs=[pl.BlockSpec(memory_space=o.memory_space) for o in outs],
        out_shape=list(outs),
        scratch_shapes=list(scratch),
        compiler_params=pltpu.CompilerParams(vmem_limit_bytes=4 << 20),
        cost_estimate=pl.CostEstimate(flops=flops, bytes_accessed=moved, transcendentals=0),
        name=name,
    )


def even_pairs(peers):
    return [(i, i ^ 1) for i in range(peers)]


def odd_pairs(peers):
    return [(i, ((i + 1) ^ 1) - 1) for i in range(1, peers - 1)] + [(0, peers - 1), (peers - 1, 0)]


def even_swap(value, axis):
    return lax.ppermute(value, axis, even_pairs(lax.axis_size(axis)))


def odd_swap(value, axis):
    return lax.ppermute(value, axis, odd_pairs(lax.axis_size(axis)))


def find_places(codes, counts, planes, out_ref):
    height, slots = codes.shape
    one = jnp.int32(1)
    step_x = jnp.where(codes >= 9, one, 0) + jnp.where(codes >= 18, one, 0)
    rest = codes - 9 * step_x
    step_y = jnp.where(rest >= 3, one, 0) + jnp.where(rest >= 6, one, 0)
    step_z = rest - 3 * step_y

    def source(step, axis):
        even_side = 2 - 2 * (lax.axis_index(axis) % 2)
        return jnp.where(step == 1, 0, jnp.where(step == even_side, one, 2))

    active = lax.broadcasted_iota(jnp.int32, (height, slots), 1) < upright(counts)
    column = source(step_y, "by") * 3 + source(step_x, "bx")
    level = lax.broadcasted_iota(jnp.int32, (height, slots), 0) + step_z - 1
    for i, size in enumerate(planes):
        out_ref[i * height : (i + 1) * height] = jnp.where(active, column * size + level, 9 * size)


def upright(row):
    size = row.shape[1]
    level = lax.broadcasted_iota(jnp.int32, (size, size), 0)
    lane = lax.broadcasted_iota(jnp.int32, (size, size), 1)
    return jnp.sum(jnp.where(level == lane, row, 0), axis=1, keepdims=True)


def places_kernel(lists_hbm, counts_hbm, after_ref, out_ref, token_ref, lists_ref, counts_ref, found_ref, sems, *, planes):
    loads = [pltpu.make_async_copy(lists_hbm, lists_ref, sems.at[0]), pltpu.make_async_copy(counts_hbm, counts_ref, sems.at[1])]
    for load in loads:
        load.start()
    for load in loads:
        load.wait()
    find_places(lists_ref[...], counts_ref[...], planes, found_ref)
    copy = pltpu.make_async_copy(found_ref, out_ref, sems.at[2])
    copy.start()
    token_ref[...] = jnp.zeros_like(token_ref)
    copy.wait()


def places(lists, counts, planes, after):
    found = (len(planes) * lists.shape[0], lists.shape[1])
    return call(
        functools.partial(places_kernel, planes=planes),
        "places",
        [HB, HB, AN],
        [pltpu.SMEM(found, jnp.int32), TOKEN],
        [
            pltpu.VMEM(lists.shape, jnp.int32),
            pltpu.VMEM(counts.shape, jnp.int32),
            pltpu.VMEM(found, jnp.int32),
            pltpu.SemaphoreType.DMA((3,)),
        ],
        moved=4 << 20,
    )(far_memory(lists), far_memory(counts), after)


def first_kernel(*refs):
    rhs_hbm, transform_hbm, inverse_hbm, slots_hbm, skel_ref, field_ref, transform_ref = refs[:7]
    rhs_ref, inverse_ref, slots_ref, sems = refs[7:]
    height, rank = inverse_ref.shape[0], inverse_ref.shape[1]
    bounds = (0, height * 3 // 8, height * 3 // 4, height)
    chunks = [slice(i, j) for i, j in zip(bounds[:-1], bounds[1:])]
    loads = [pltpu.make_async_copy(transform_hbm.at[c], transform_ref.at[c], sems.at[i]) for i, c in enumerate(chunks)]
    rhs_load = pltpu.make_async_copy(rhs_hbm, rhs_ref, sems.at[3])
    inverse_load = pltpu.make_async_copy(inverse_hbm, inverse_ref, sems.at[4])
    slots_load = pltpu.make_async_copy(slots_hbm, slots_ref, sems.at[5])
    for copy in (rhs_load, *loads, inverse_load, slots_load):
        copy.start()
    rhs_load.wait()
    redundant = []
    for c, load in zip(chunks, loads):
        load.wait()
        boxes = range(c.start, c.stop)
        projected = [jnp.dot(rhs_ref[z], transform_ref[z], preferred_element_type=F32) for z in boxes]
        for z, rows in zip(boxes, projected):
            skel_ref[z] = rows[:, rank:]
            redundant.append(rows[:, :rank].astype(BF))
    inverse_load.wait()
    for z in range(height):
        field_ref[z] = jnp.dot(redundant[z], inverse_ref[z], preferred_element_type=F32).astype(BF)
    slots_load.wait()
    plane = jnp.broadcast_to(upright(slots_ref[...]), (height, rank)).astype(F32)
    plane = jnp.concatenate([plane, jnp.zeros((field_ref.shape[1] - height, rank), F32)], axis=0)
    field_ref[height] = plane.astype(BF)


def first(right_sides, transform, inverse, slots):
    height, rhs_count, points = right_sides.shape
    rank = inverse.shape[1]
    operands = (right_sides, transform, inverse, slots)
    return call(
        first_kernel,
        "first",
        [HB] * 4,
        [
            pltpu.VMEM((height, rhs_count, rank), F32),
            pltpu.VMEM((height + 1, rhs_count, rank), BF),
            pltpu.VMEM(transform.shape, BF),
        ],
        [
            pltpu.VMEM(right_sides.shape, BF),
            pltpu.VMEM(inverse.shape, BF),
            pltpu.VMEM(slots.shape, jnp.int32),
            pltpu.SemaphoreType.DMA((6,)),
        ],
    )(*map(far_memory, operands))


def fetch_kernel(value_hbm, after_ref, out_ref, token_ref, sem, *, start):
    copy = pltpu.make_async_copy(value_hbm.at[start : start + out_ref.shape[0]], out_ref, sem)
    copy.start()
    token_ref[...] = jnp.zeros_like(token_ref)
    copy.wait()


def fetch(value, after, start, stop):
    shape = (stop - start, *value.shape[1:])
    return call(
        functools.partial(fetch_kernel, start=start),
        "fetch",
        [HB, AN],
        [pltpu.VMEM(shape, value.dtype), TOKEN],
        [pltpu.SemaphoreType.DMA],
        moved=4 * math.prod(shape),
    )(far_memory(value), after)


def pack_kernel(*refs):
    out_ref = refs[-1]
    planes = refs[0].shape[0]
    for i in range(out_ref.shape[0] // planes):
        out_ref[i * planes : (i + 1) * planes] = refs[i][...]


def pack(parts, after):
    planes, rows, cols = parts[0].shape
    shape = pltpu.VMEM((len(parts) * planes, rows, cols), BF)
    return call(pack_kernel, "pack", [VM] * len(parts) + [AN] * len(after), [shape])(*map(resident, parts), *after)[0]


def fill_table(table_ref, parts):
    at = 0
    for part in parts:
        table_ref[at : at + part.shape[0]] = part[...]
        at += part.shape[0]
    table_ref[at] = jnp.zeros(table_ref.shape[1:], BF)


def coupling(table_ref, where_ref, row, fill_ref, z):
    slots, rank = fill_ref.shape[1], fill_ref.shape[2]
    rows = jnp.concatenate([table_ref[where_ref[row, k]] for k in range(slots)], axis=1)
    blocks = fill_ref[z].reshape(slots * rank, fill_ref.shape[3])
    return jnp.dot(rows, blocks, preferred_element_type=F32)


def lower_kernel(*refs):
    parts, refs = refs[1:7], refs[:1] + refs[7:]
    where_ref, skel_ref, fill_ref, after_ref, out_ref, child_ref, table_ref, child_vmem, sem = refs
    height, planes = out_ref.shape[0], parts[1].shape[0]
    lane = lax.broadcasted_iota(jnp.int32, child_vmem.shape, 1)
    level = lax.broadcasted_iota(jnp.int32, child_vmem.shape, 0)
    found = jnp.zeros(child_vmem.shape, jnp.int32)
    columns = [part[at] for part in (parts[0], parts[2]) for at in (height, planes + height)]
    for i, column in enumerate(columns):
        slots = column.astype(F32)[:height].astype(jnp.int32)
        found = found + jnp.where(slots == lane, i * height + level, 0)
    child_vmem[...] = found
    copy = pltpu.make_async_copy(child_vmem, child_ref, sem)
    copy.start()
    fill_table(table_ref, parts)
    for z in range(height):
        out_ref[z] = (skel_ref[z] - coupling(table_ref, where_ref, z, fill_ref, z)).astype(BF)
    copy.wait()


def lower(where, parts, skel, fill, after):
    height, rhs_count, rank = skel.shape
    planes = sum(part.shape[0] for part in parts) + 1
    return call(
        lower_kernel,
        "lower",
        [SM] + [VM] * 8 + [AN],
        [pltpu.VMEM((height, rhs_count, rank), BF), pltpu.SMEM((height, rank), jnp.int32)],
        [
            pltpu.VMEM((planes, rhs_count, rank), BF),
            pltpu.VMEM((height, rank), jnp.int32),
            pltpu.SemaphoreType.DMA,
        ],
    )(scalars(where), *map(resident, (*parts, skel, fill)), after)


def parent_kernel(child_ref, own_ref, far_ref, rows_ref, out_ref, table_ref):
    planes = own_ref.shape[0]
    table_ref[0:planes] = own_ref[...]
    table_ref[planes : 2 * planes] = far_ref[...]
    for i in range(out_ref.shape[0] // 2):
        places = [child_ref[2 * i, s] + child_ref[2 * i + 1, s] for s in range(8)]
        stacked = jnp.concatenate([table_ref[place] for place in places], axis=1)
        for z in (2 * i, 2 * i + 1):
            out_ref[z] = jnp.dot(stacked, rows_ref[z], preferred_element_type=F32).astype(BF)


def parent(child, own, far, rows):
    height, rhs_count, rank = rows.shape[0], own.shape[1], own.shape[2]
    return call(
        parent_kernel,
        "parent",
        [SM, VM, VM, VM],
        [pltpu.VMEM((height, rhs_count, rank), BF)],
        [pltpu.VMEM((2 * own.shape[0], rhs_count, rank), BF)],
    )(scalars(child), resident(own), resident(far), resident(rows))[0]


LAST = (((1,), (1,)), ((), ()))


def half_kernel(skel_ref, transform_ref, out_ref, token_ref):
    rank = skel_ref.shape[2]
    for z in range(out_ref.shape[0]):
        out_ref[z] = lax.dot_general(skel_ref[z], transform_ref[z, :, rank:], LAST, preferred_element_type=F32)
    token_ref[...] = jnp.zeros_like(token_ref)


def half(skel, transform):
    height, rhs_count, rank = skel.shape
    shape = pltpu.VMEM((height, rhs_count, transform.shape[1]), F32)
    return call(half_kernel, "half", [VM, VM], [shape, TOKEN], moved=4 << 20)(resident(skel), resident(transform))


def upper_kernel(*refs):
    parts, refs = refs[1:7], refs[:1] + refs[7:]
    where_ref, base_ref, local_ref, low_ref, high_ref, transform_ref, out_hbm, table_ref, red_ref, out_ref, sems = refs
    fill_table(table_ref, parts)
    height, rank = out_ref.shape[0], local_ref.shape[2]
    for z in range(height):
        fill_ref, at = (low_ref, z) if z < low_ref.shape[0] else (high_ref, z - low_ref.shape[0])
        backward = coupling(table_ref, where_ref, height + z, fill_ref, at)
        red_ref[z] = (local_ref[z].astype(F32) - backward).astype(BF)
    copies = []
    block = height // sems.shape[0]
    for z in range(height):
        solved = lax.dot_general(red_ref[z], transform_ref[z, :, :rank], LAST, preferred_element_type=F32)
        out_ref[z] = (solved + base_ref[z]).astype(BF)
        if (z + 1) % block == 0:
            part = slice(z + 1 - block, z + 1)
            copies.append(pltpu.make_async_copy(out_ref.at[part], out_hbm.at[part], sems.at[z // block]))
            copies[-1].start()
    for copy in copies:
        copy.wait()


def upper(where, parts, base, local, low, high, transform):
    height, rhs_count, points = base.shape
    rank = local.shape[2]
    planes = sum(part.shape[0] for part in parts) + 1
    return call(
        upper_kernel,
        "upper",
        [SM] + [VM] * 11,
        [pltpu.HBM((height, rhs_count, points), BF)],
        [
            pltpu.VMEM((planes, rhs_count, rank), BF),
            pltpu.VMEM((height, rhs_count, rank), BF),
            pltpu.VMEM((height, rhs_count, points), BF),
            pltpu.SemaphoreType.DMA((2,)),
        ],
    )(scalars(where), *map(resident, (*parts, base, local, low, high, transform)))[0]


def halo(field, before, between):
    odd = odd_swap(field, "bx")
    even = even_swap(field, "bx")
    near = pack([field, even], before)
    tokens = between(near)
    if tokens:
        odd = pack([odd], tokens)
    parts = [near, odd]
    for swap in (even_swap, odd_swap):
        parts += [swap(near, "by"), swap(odd, "by")]
    return parts


def body(right_sides, transform, inverse, fill_lower, fill_upper, parent_rows, neighbours, counts, child_slot):
    height = right_sides.shape[2]
    skel, field, transform = first(right_sides[0, 0], transform[0, 0], inverse[0, 0], child_slot[0])
    found = []

    def between(near):
        found.extend(places(neighbours[0, 0], counts[0], (height + 1, height), near))
        return found[1:]

    parts = halo(field, [], between)
    where = found[0]
    fill, _ = fetch(fill_lower[0, 0], parts[1], 0, height)
    reduced, child = lower(where, parts, skel, fill, field)
    rows, rows_token = fetch(parent_rows[0, 0], reduced, 0, height)
    low, low_token = fetch(fill_upper[0, 0], reduced, 0, height // 2)
    pair = pack([reduced, even_swap(reduced, "bx")], [rows_token, low_token])
    skel_sol = parent(child, pair, even_swap(pair, "by"), rows)
    base, base_token = half(skel_sol, transform)
    high = []

    def between(near):
        value, token = fetch(fill_upper[0, 0], near, height // 2, height)
        high.append(value)
        return [token]

    parts = halo(skel_sol, [base_token], between)
    solved = upper(where, parts, base, field, low, high[0], transform)
    return solved[None, None]


def solution(mesh):
    wide = P("bx", "by", None, None, None)
    placed = (wide, wide, wide, P("bx", "by", None, None, None, None), P("bx", "by", None, None, None, None), wide)
    placed = placed + (P("bx", "by", None, None), P("bx", "by", None), P("bx", "by", None))
    return jax.shard_map(body, mesh=mesh, in_specs=placed, out_specs=wide, check_vma=False)
```

```python
import functools
import math

import jax
import jax.numpy as jnp
from jax import lax
from jax.experimental import pallas as pl
from jax.experimental.pallas import tpu as pltpu
from jax.sharding import PartitionSpec as P

BF = jnp.bfloat16
F32 = jnp.float32
VM = pl.BlockSpec(memory_space=pltpu.VMEM)
SM = pl.BlockSpec(memory_space=pltpu.SMEM)
HB = pl.BlockSpec(memory_space=pltpu.HBM)
AN = pl.BlockSpec(memory_space=pl.ANY)
TOKEN = pltpu.VMEM((8, 128), F32)


def resident(value):
    return pltpu.with_memory_space_constraint(value, pltpu.VMEM)


def far_memory(value):
    return pltpu.with_memory_space_constraint(value, pltpu.HBM)


def scalars(value):
    return pltpu.with_memory_space_constraint(value, pltpu.SMEM)


def call(kernel, name, ins, outs, scratch=(), moved=0, flops=0):
    return pl.pallas_call(
        kernel,
        in_specs=ins,
        out_specs=[pl.BlockSpec(memory_space=o.memory_space) for o in outs],
        out_shape=list(outs),
        scratch_shapes=list(scratch),
        compiler_params=pltpu.CompilerParams(vmem_limit_bytes=4 << 20),
        cost_estimate=pl.CostEstimate(flops=flops, bytes_accessed=moved, transcendentals=0),
        name=name,
    )


def even_pairs(peers):
    return [(i, i ^ 1) for i in range(peers)]


def odd_pairs(peers):
    return [(i, ((i + 1) ^ 1) - 1) for i in range(1, peers - 1)] + [(0, peers - 1), (peers - 1, 0)]


def even_swap(value, axis):
    return lax.ppermute(value, axis, even_pairs(lax.axis_size(axis)))


def odd_swap(value, axis):
    return lax.ppermute(value, axis, odd_pairs(lax.axis_size(axis)))


def find_places(codes, counts, planes, out_ref):
    height, slots = codes.shape
    one = jnp.int32(1)
    step_x = jnp.where(codes >= 9, one, 0) + jnp.where(codes >= 18, one, 0)
    rest = codes - 9 * step_x
    step_y = jnp.where(rest >= 3, one, 0) + jnp.where(rest >= 6, one, 0)
    step_z = rest - 3 * step_y

    def source(step, axis):
        even_side = 2 - 2 * (lax.axis_index(axis) % 2)
        return jnp.where(step == 1, 0, jnp.where(step == even_side, one, 2))

    lane = lax.broadcasted_iota(jnp.int32, (height, slots), 1)
    column = source(step_y, "by") * 3 + source(step_x, "bx")
    level = lax.broadcasted_iota(jnp.int32, (height, slots), 0) + step_z - 1
    active = lane < upright(counts)
    early = active & (column != 5) & (column != 8)
    table_column = column - jnp.where(column > 5, one, 0)
    for i, size in enumerate(planes):
        out_ref[i * height : (i + 1) * height] = jnp.where(early, table_column * size + level, 7 * size)
    late = jnp.full((height, slots), -one)
    for i, late_column in enumerate((5, 8)):
        for step in range(3):
            hit = active & (column == late_column) & (step_z == step)
            slot = jnp.sum(jnp.where(hit, lane + 1, 0), axis=1, keepdims=True) - 1
            late = jnp.where(lane == 3 * i + step, slot, late)
    out_ref[len(planes) * height :] = late


def upright(row):
    size = row.shape[1]
    level = lax.broadcasted_iota(jnp.int32, (size, size), 0)
    lane = lax.broadcasted_iota(jnp.int32, (size, size), 1)
    return jnp.sum(jnp.where(level == lane, row, 0), axis=1, keepdims=True)


def places_kernel(lists_hbm, counts_hbm, value_hbm, after_ref, out_ref, token_ref, value_ref, *scratch, planes):
    lists_ref, counts_ref, found_ref, sems = scratch
    loads = [pltpu.make_async_copy(lists_hbm, lists_ref, sems.at[0]), pltpu.make_async_copy(counts_hbm, counts_ref, sems.at[1])]
    value_load = pltpu.make_async_copy(value_hbm.at[0 : value_ref.shape[0]], value_ref, sems.at[3])
    for load in loads:
        load.start()
    value_load.start()
    for load in loads:
        load.wait()
    find_places(lists_ref[...], counts_ref[...], planes, found_ref)
    copy = pltpu.make_async_copy(found_ref, out_ref, sems.at[2])
    copy.start()
    token_ref[...] = jnp.zeros_like(token_ref)
    value_load.wait()
    copy.wait()


def places(lists, counts, planes, value, boxes, after):
    found = ((len(planes) + 1) * lists.shape[0], lists.shape[1])
    return call(
        functools.partial(places_kernel, planes=planes),
        "places",
        [HB, HB, HB, AN],
        [pltpu.SMEM(found, jnp.int32), TOKEN, pltpu.VMEM((boxes, *value.shape[1:]), BF)],
        [
            pltpu.VMEM(lists.shape, jnp.int32),
            pltpu.VMEM(counts.shape, jnp.int32),
            pltpu.VMEM(found, jnp.int32),
            pltpu.SemaphoreType.DMA((4,)),
        ],
        moved=4 << 20,
    )(far_memory(lists), far_memory(counts), far_memory(value), after)


def first_kernel(*refs):
    rhs_hbm, transform_hbm, inverse_hbm, slots_hbm, skel_ref, field_ref, transform_ref = refs[:7]
    rhs_ref, inverse_ref, slots_ref, sems = refs[7:]
    height, rank = inverse_ref.shape[0], inverse_ref.shape[1]
    bounds = (0, height * 3 // 8, height * 3 // 4, height)
    chunks = [slice(i, j) for i, j in zip(bounds[:-1], bounds[1:])]
    loads = [pltpu.make_async_copy(transform_hbm.at[c], transform_ref.at[c], sems.at[i]) for i, c in enumerate(chunks)]
    rhs_load = pltpu.make_async_copy(rhs_hbm, rhs_ref, sems.at[3])
    inverse_load = pltpu.make_async_copy(inverse_hbm, inverse_ref, sems.at[4])
    slots_load = pltpu.make_async_copy(slots_hbm, slots_ref, sems.at[5])
    for copy in (rhs_load, *loads, inverse_load, slots_load):
        copy.start()
    rhs_load.wait()
    redundant = []
    for c, load in zip(chunks, loads):
        load.wait()
        boxes = range(c.start, c.stop)
        projected = [jnp.dot(rhs_ref[z], transform_ref[z], preferred_element_type=F32) for z in boxes]
        for z, rows in zip(boxes, projected):
            skel_ref[z] = rows[:, rank:]
            redundant.append(rows[:, :rank].astype(BF))
    inverse_load.wait()
    for z in range(height):
        field_ref[z] = jnp.dot(redundant[z], inverse_ref[z], preferred_element_type=F32).astype(BF)
    slots_load.wait()
    plane = jnp.broadcast_to(upright(slots_ref[...]), (height, rank)).astype(F32)
    plane = jnp.concatenate([plane, jnp.zeros((field_ref.shape[1] - height, rank), F32)], axis=0)
    field_ref[height] = plane.astype(BF)


def first(right_sides, transform, inverse, slots):
    height, rhs_count, points = right_sides.shape
    rank = inverse.shape[1]
    operands = (right_sides, transform, inverse, slots)
    return call(
        first_kernel,
        "first",
        [HB] * 4,
        [
            pltpu.VMEM((height, rhs_count, rank), F32),
            pltpu.VMEM((height + 1, rhs_count, rank), BF),
            pltpu.VMEM(transform.shape, BF),
        ],
        [
            pltpu.VMEM(right_sides.shape, BF),
            pltpu.VMEM(inverse.shape, BF),
            pltpu.VMEM(slots.shape, jnp.int32),
            pltpu.SemaphoreType.DMA((6,)),
        ],
    )(*map(far_memory, operands))


def fetch_kernel(value_hbm, after_ref, out_ref, token_ref, sem, *, start):
    copy = pltpu.make_async_copy(value_hbm.at[start : start + out_ref.shape[0]], out_ref, sem)
    copy.start()
    token_ref[...] = jnp.zeros_like(token_ref)
    copy.wait()


def fetch(value, after, start, stop):
    shape = (stop - start, *value.shape[1:])
    return call(
        functools.partial(fetch_kernel, start=start),
        "fetch",
        [HB, AN],
        [pltpu.VMEM(shape, value.dtype), TOKEN],
        [pltpu.SemaphoreType.DMA],
        moved=4 * math.prod(shape),
    )(far_memory(value), after)


def pack_kernel(*refs):
    out_ref = refs[-1]
    planes = refs[0].shape[0]
    for i in range(out_ref.shape[0] // planes):
        out_ref[i * planes : (i + 1) * planes] = refs[i][...]


def pack(parts, after):
    planes, rows, cols = parts[0].shape
    shape = pltpu.VMEM((len(parts) * planes, rows, cols), BF)
    return call(pack_kernel, "pack", [VM] * len(parts) + [AN] * len(after), [shape])(*map(resident, parts), *after)[0]


def fill_table(table_ref, parts):
    at = 0
    for part in parts:
        table_ref[at : at + part.shape[0]] = part[...]
        at += part.shape[0]
    table_ref[at] = jnp.zeros(table_ref.shape[1:], BF)


def coupling(table_ref, where_ref, row, blocks_ref):
    slots, rank = blocks_ref.shape[0], blocks_ref.shape[1]
    rows = jnp.concatenate([table_ref[where_ref[row, k]] for k in range(slots)], axis=1)
    return jnp.dot(rows, blocks_ref[...].reshape(slots * rank, rank), preferred_element_type=F32)


def late_coupling(columns, where_ref, row, blocks_ref, z, height):
    rows, blocks = [], []
    for i, column_ref in enumerate(columns):
        for step in range(3):
            if 0 <= z + step - 1 < height:
                slot = where_ref[row, 3 * i + step]
                plane = column_ref[z + step - 1]
                rows.append(jnp.where(slot >= 0, plane, jnp.zeros_like(plane)))
                blocks.append(blocks_ref[jnp.maximum(slot, 0)])
    return jnp.dot(jnp.concatenate(rows, axis=1), jnp.concatenate(blocks, axis=0), preferred_element_type=F32)


def early_lower_kernel(*refs):
    where_ref, parts, refs = refs[0], [refs[i] for i in (4, 3, 2, 1)], refs[5:]
    skel_ref, low_ref, fill_hbm, out_ref, child_ref, high_ref, table_ref, child_vmem, sems = refs
    height, planes, done = out_ref.shape[0], parts[1].shape[0], low_ref.shape[0]
    block = high_ref.shape[0] // (sems.shape[0] - 1)
    loads = []
    for i in range(sems.shape[0] - 1):
        source = fill_hbm.at[done + i * block : done + (i + 1) * block]
        loads.append(pltpu.make_async_copy(source, high_ref.at[i * block : (i + 1) * block], sems.at[i]))
        loads[-1].start()
    lane = lax.broadcasted_iota(jnp.int32, child_vmem.shape, 1)
    level = lax.broadcasted_iota(jnp.int32, child_vmem.shape, 0)
    found = jnp.zeros(child_vmem.shape, jnp.int32)
    columns = [part[at] for part in (parts[0], parts[2]) for at in (height, planes + height)]
    for i, column in enumerate(columns):
        slots = column.astype(F32)[:height].astype(jnp.int32)
        found = found + jnp.where(slots == lane, i * height + level, 0)
    child_vmem[...] = found
    copy = pltpu.make_async_copy(child_vmem, child_ref, sems.at[len(loads)])
    copy.start()
    fill_table(table_ref, parts)
    for z in range(height):
        if z >= done and (z - done) % block == 0:
            loads[(z - done) // block].wait()
        blocks_ref = low_ref.at[z] if z < done else high_ref.at[z - done]
        out_ref[z] = skel_ref[z] - coupling(table_ref, where_ref, z, blocks_ref)
    copy.wait()


def early_lower(where, parts, skel, low, fill):
    height, rhs_count, rank = skel.shape
    planes = sum(part.shape[0] for part in parts) + 1
    return call(
        early_lower_kernel,
        "early_lower",
        [SM] + [VM] * 6 + [HB],
        [
            pltpu.VMEM((height, rhs_count, rank), F32),
            pltpu.SMEM((height, rank), jnp.int32),
            pltpu.VMEM((height - low.shape[0], *fill.shape[1:]), BF),
        ],
        [
            pltpu.VMEM((planes, rhs_count, rank), BF),
            pltpu.VMEM((height, rank), jnp.int32),
            pltpu.SemaphoreType.DMA((5,)),
        ],
        moved=16 << 20,
    )(scalars(where), *map(resident, (*parts[::-1], skel, low)), far_memory(fill))


def late_lower_kernel(where_ref, odd_ref, even_ref, base_ref, low_ref, high_ref, out_ref):
    height, done = out_ref.shape[0], low_ref.shape[0]
    for z in range(height):
        blocks_ref = low_ref.at[z] if z < done else high_ref.at[z - done]
        out_ref[z] = (base_ref[z] - late_coupling((even_ref, odd_ref), where_ref, 2 * height + z, blocks_ref, z, height)).astype(BF)


def late_lower(where, columns, base, low, high):
    shape = pltpu.VMEM(base.shape, BF)
    operands = (*columns[::-1], base, low, high)
    return call(late_lower_kernel, "late_lower", [SM] + [VM] * 5, [shape])(scalars(where), *map(resident, operands))[0]


def parent_kernel(child_ref, own_ref, far_ref, rows_ref, out_ref, table_ref):
    planes = own_ref.shape[0]
    table_ref[0:planes] = own_ref[...]
    table_ref[planes : 2 * planes] = far_ref[...]
    for i in range(out_ref.shape[0] // 2):
        places = [child_ref[2 * i, s] + child_ref[2 * i + 1, s] for s in range(8)]
        stacked = jnp.concatenate([table_ref[place] for place in places], axis=1)
        for z in (2 * i, 2 * i + 1):
            out_ref[z] = jnp.dot(stacked, rows_ref[z], preferred_element_type=F32).astype(BF)


def parent(child, own, far, rows):
    height, rhs_count, rank = rows.shape[0], own.shape[1], own.shape[2]
    return call(
        parent_kernel,
        "parent",
        [SM, VM, VM, VM],
        [pltpu.VMEM((height, rhs_count, rank), BF)],
        [pltpu.VMEM((2 * own.shape[0], rhs_count, rank), BF)],
    )(scalars(child), resident(own), resident(far), resident(rows))[0]


LAST = (((1,), (1,)), ((), ()))


def half_kernel(skel_ref, transform_ref, out_ref, token_ref):
    rank = skel_ref.shape[2]
    for z in range(out_ref.shape[0]):
        out_ref[z] = lax.dot_general(skel_ref[z], transform_ref[z, :, rank:], LAST, preferred_element_type=F32)
    token_ref[...] = jnp.zeros_like(token_ref)


def half(skel, transform):
    height, rhs_count, rank = skel.shape
    shape = pltpu.VMEM((height, rhs_count, transform.shape[1]), F32)
    return call(half_kernel, "half", [VM, VM], [shape, TOKEN], moved=4 << 20)(resident(skel), resident(transform))


def early_upper_kernel(*refs):
    where_ref, parts, refs = refs[0], [refs[i] for i in (4, 3, 2, 1)], refs[5:]
    local_ref, low_ref, high_ref, out_ref, table_ref = refs
    fill_table(table_ref, parts)
    height, done = out_ref.shape[0], low_ref.shape[0]
    for z in range(height):
        blocks_ref = low_ref.at[z] if z < done else high_ref.at[z - done]
        out_ref[z] = local_ref[z].astype(F32) - coupling(table_ref, where_ref, height + z, blocks_ref)


def early_upper(where, parts, local, low, high):
    height, rhs_count, rank = parts[1].shape
    planes = sum(part.shape[0] for part in parts) + 1
    return call(
        early_upper_kernel,
        "early_upper",
        [SM] + [VM] * 7,
        [pltpu.VMEM((height, rhs_count, rank), F32)],
        [pltpu.VMEM((planes, rhs_count, rank), BF)],
        moved=16 << 20,
    )(scalars(where), *map(resident, (*parts[::-1], local, low, high)))[0]


def late_upper_kernel(where_ref, odd_ref, even_ref, base_ref, solved_ref, low_ref, high_ref, transform_ref, out_hbm, red_ref, out_ref, sems):
    height, rank, done = base_ref.shape[0], base_ref.shape[2], low_ref.shape[0]
    for z in range(height):
        blocks_ref = low_ref.at[z] if z < done else high_ref.at[z - done]
        backward = late_coupling((even_ref, odd_ref), where_ref, 2 * height + z, blocks_ref, z, height)
        red_ref[z] = (base_ref[z] - backward).astype(BF)
    copies = []
    block = height // sems.shape[0]
    for z in range(height):
        solved = lax.dot_general(red_ref[z], transform_ref[z, :, :rank], LAST, preferred_element_type=F32)
        out_ref[z] = (solved + solved_ref[z]).astype(BF)
        if (z + 1) % block == 0:
            part = slice(z + 1 - block, z + 1)
            copies.append(pltpu.make_async_copy(out_ref.at[part], out_hbm.at[part], sems.at[z // block]))
            copies[-1].start()
    for copy in copies:
        copy.wait()


def late_upper(where, columns, base, solved, low, high, transform):
    operands = (*columns[::-1], base, solved, low, high, transform)
    return call(
        late_upper_kernel,
        "late_upper",
        [SM] + [VM] * 7,
        [pltpu.HBM(solved.shape, BF)],
        [pltpu.VMEM(base.shape, BF), pltpu.VMEM(solved.shape, BF), pltpu.SemaphoreType.DMA((2,))],
    )(scalars(where), *map(resident, operands))[0]


def halo(field, before, between):
    odd = odd_swap(field, "bx")
    even = even_swap(field, "bx")
    near = pack([field, even], before)
    tokens = between(near)
    odd = pack([odd], tokens)
    for _ in range(3):
        odd = pack([odd], [])
    early = [near, odd, even_swap(near, "by"), odd_swap(near, "by")]
    return early, [even_swap(odd, "by"), odd_swap(odd, "by")]


def body(right_sides, transform, inverse, fill_lower, fill_upper, parent_rows, neighbours, counts, child_slot):
    height = right_sides.shape[2]
    skel, field, transform = first(right_sides[0, 0], transform[0, 0], inverse[0, 0], child_slot[0])
    found = []

    def between(near):
        found.extend(places(neighbours[0, 0], counts[0], (height + 1, height), fill_lower[0, 0], height // 4, near))
        return found[1:2]

    early, late = halo(field, [], between)
    where, _, low = found
    base, child, high = early_lower(where, early, skel, low, fill_lower[0, 0])
    reduced = late_lower(where, late, base, low, high)
    rows, rows_token = fetch(parent_rows[0, 0], reduced, 0, height)
    low, low_token = fetch(fill_upper[0, 0], reduced, 0, height // 2)
    pair = pack([reduced, even_swap(reduced, "bx")], [rows_token, low_token])
    skel_sol = parent(child, pair, even_swap(pair, "by"), rows)
    solved, solved_token = half(skel_sol, transform)
    high = []

    def between(near):
        value, token = fetch(fill_upper[0, 0], near, height // 2, height)
        high.append(value)
        return [token]

    early, late = halo(skel_sol, [solved_token], between)
    base = early_upper(where, early, field, low, high[0])
    solved = late_upper(where, late, base, solved, low, high[0], transform)
    return solved[None, None]


def solution(mesh):
    wide = P("bx", "by", None, None, None)
    placed = (wide, wide, wide, P("bx", "by", None, None, None, None), P("bx", "by", None, None, None, None), wide)
    placed = placed + (P("bx", "by", None, None), P("bx", "by", None), P("bx", "by", None))
    return jax.shard_map(body, mesh=mesh, in_specs=placed, out_specs=wide, check_vma=False)
```

```python
import functools
import math

import jax
import jax.numpy as jnp
from jax import lax
from jax.experimental import pallas as pl
from jax.experimental.pallas import tpu as pltpu
from jax.sharding import PartitionSpec as P

BF = jnp.bfloat16
F32 = jnp.float32
VM = pl.BlockSpec(memory_space=pltpu.VMEM)
SM = pl.BlockSpec(memory_space=pltpu.SMEM)
HB = pl.BlockSpec(memory_space=pltpu.HBM)
AN = pl.BlockSpec(memory_space=pl.ANY)
TOKEN = pltpu.VMEM((8, 128), F32)


def resident(value):
    return pltpu.with_memory_space_constraint(value, pltpu.VMEM)


def far_memory(value):
    return pltpu.with_memory_space_constraint(value, pltpu.HBM)


def scalars(value):
    return pltpu.with_memory_space_constraint(value, pltpu.SMEM)


def call(kernel, name, ins, outs, scratch=(), moved=0, flops=0):
    return pl.pallas_call(
        kernel,
        in_specs=ins,
        out_specs=[pl.BlockSpec(memory_space=o.memory_space) for o in outs],
        out_shape=list(outs),
        scratch_shapes=list(scratch),
        compiler_params=pltpu.CompilerParams(vmem_limit_bytes=4 << 20),
        cost_estimate=pl.CostEstimate(flops=flops, bytes_accessed=moved, transcendentals=0),
        name=name,
    )


def even_pairs(peers):
    return [(i, i ^ 1) for i in range(peers)]


def even_swap(value, axis):
    return lax.ppermute(value, axis, even_pairs(lax.axis_size(axis)))


def odd_swap(value, axis):
    across, along = lax.axis_size("bx"), lax.axis_size("by")

    def other(i, peers):
        return ((i + 1) ^ 1) - 1 if 0 < i < peers - 1 else None

    pairs = []
    for i in range(across):
        for j in range(along):
            if axis == "bx":
                to = other(i, across)
                to = (i, j ^ 1) if to is None else (to, j)
            else:
                to = other(j, along)
                to = (i ^ 1, j) if to is None else (i, to)
            pairs.append((i * along + j, to[0] * along + to[1]))
    return lax.ppermute(value, ("bx", "by"), pairs)


def find_places(codes, counts, planes, out_ref):
    height, slots = codes.shape
    one = jnp.int32(1)
    step_x = jnp.where(codes >= 9, one, 0) + jnp.where(codes >= 18, one, 0)
    rest = codes - 9 * step_x
    step_y = jnp.where(rest >= 3, one, 0) + jnp.where(rest >= 6, one, 0)
    step_z = rest - 3 * step_y

    def source(step, axis):
        even_side = 2 - 2 * (lax.axis_index(axis) % 2)
        return jnp.where(step == 1, 0, jnp.where(step == even_side, one, 2))

    lane = lax.broadcasted_iota(jnp.int32, (height, slots), 1)
    column = source(step_y, "by") * 3 + source(step_x, "bx")
    level = lax.broadcasted_iota(jnp.int32, (height, slots), 0) + step_z - 1
    active = lane < upright(counts)
    early = active & (column != 5) & (column != 8)
    table_column = column - jnp.where(column > 5, one, 0)
    for i, size in enumerate(planes):
        out_ref[i * height : (i + 1) * height] = jnp.where(early, table_column * size + level, 7 * size)
    late = jnp.full((height, slots), -one)
    for i, late_column in enumerate((5, 8)):
        for step in range(3):
            hit = active & (column == late_column) & (step_z == step)
            slot = jnp.sum(jnp.where(hit, lane + 1, 0), axis=1, keepdims=True) - 1
            late = jnp.where(lane == 3 * i + step, slot, late)
    out_ref[len(planes) * height :] = late


def upright(row):
    size = row.shape[1]
    level = lax.broadcasted_iota(jnp.int32, (size, size), 0)
    lane = lax.broadcasted_iota(jnp.int32, (size, size), 1)
    return jnp.sum(jnp.where(level == lane, row, 0), axis=1, keepdims=True)


def places_kernel(lists_hbm, counts_hbm, value_hbm, after_ref, out_ref, token_ref, value_ref, *scratch, planes):
    lists_ref, counts_ref, found_ref, sems = scratch
    loads = [pltpu.make_async_copy(lists_hbm, lists_ref, sems.at[0]), pltpu.make_async_copy(counts_hbm, counts_ref, sems.at[1])]
    value_load = pltpu.make_async_copy(value_hbm.at[0 : value_ref.shape[0]], value_ref, sems.at[3])
    for load in loads:
        load.start()
    value_load.start()
    for load in loads:
        load.wait()
    find_places(lists_ref[...], counts_ref[...], planes, found_ref)
    copy = pltpu.make_async_copy(found_ref, out_ref, sems.at[2])
    copy.start()
    token_ref[...] = jnp.zeros_like(token_ref)
    value_load.wait()
    copy.wait()


def places(lists, counts, planes, value, boxes, after):
    found = ((len(planes) + 1) * lists.shape[0], lists.shape[1])
    return call(
        functools.partial(places_kernel, planes=planes),
        "places",
        [HB, HB, HB, AN],
        [pltpu.SMEM(found, jnp.int32), TOKEN, pltpu.VMEM((boxes, *value.shape[1:]), BF)],
        [
            pltpu.VMEM(lists.shape, jnp.int32),
            pltpu.VMEM(counts.shape, jnp.int32),
            pltpu.VMEM(found, jnp.int32),
            pltpu.SemaphoreType.DMA((4,)),
        ],
        moved=4 << 20,
    )(far_memory(lists), far_memory(counts), far_memory(value), after)


def first_kernel(*refs):
    rhs_hbm, transform_hbm, inverse_hbm, slots_hbm, skel_ref, field_ref, transform_ref = refs[:7]
    rhs_ref, inverse_ref, slots_ref, sems = refs[7:]
    height, rank = inverse_ref.shape[0], inverse_ref.shape[1]
    bounds = (0, height * 3 // 8, height * 3 // 4, height)
    chunks = [slice(i, j) for i, j in zip(bounds[:-1], bounds[1:])]
    loads = [pltpu.make_async_copy(transform_hbm.at[c], transform_ref.at[c], sems.at[i]) for i, c in enumerate(chunks)]
    rhs_load = pltpu.make_async_copy(rhs_hbm, rhs_ref, sems.at[3])
    inverse_load = pltpu.make_async_copy(inverse_hbm, inverse_ref, sems.at[4])
    slots_load = pltpu.make_async_copy(slots_hbm, slots_ref, sems.at[5])
    for copy in (rhs_load, *loads, inverse_load, slots_load):
        copy.start()
    rhs_load.wait()
    redundant = []
    for c, load in zip(chunks, loads):
        load.wait()
        boxes = range(c.start, c.stop)
        projected = [jnp.dot(rhs_ref[z], transform_ref[z], preferred_element_type=F32) for z in boxes]
        for z, rows in zip(boxes, projected):
            skel_ref[z] = rows[:, rank:]
            redundant.append(rows[:, :rank].astype(BF))
    inverse_load.wait()
    for z in range(height):
        field_ref[z] = jnp.dot(redundant[z], inverse_ref[z], preferred_element_type=F32).astype(BF)
    slots_load.wait()
    plane = jnp.broadcast_to(upright(slots_ref[...]), (height, rank)).astype(F32)
    plane = jnp.concatenate([plane, jnp.zeros((field_ref.shape[1] - height, rank), F32)], axis=0)
    field_ref[height] = plane.astype(BF)


def first(right_sides, transform, inverse, slots):
    height, rhs_count, points = right_sides.shape
    rank = inverse.shape[1]
    operands = (right_sides, transform, inverse, slots)
    return call(
        first_kernel,
        "first",
        [HB] * 4,
        [
            pltpu.VMEM((height, rhs_count, rank), F32),
            pltpu.VMEM((height + 1, rhs_count, rank), BF),
            pltpu.VMEM(transform.shape, BF),
        ],
        [
            pltpu.VMEM(right_sides.shape, BF),
            pltpu.VMEM(inverse.shape, BF),
            pltpu.VMEM(slots.shape, jnp.int32),
            pltpu.SemaphoreType.DMA((6,)),
        ],
    )(*map(far_memory, operands))


def fetch_kernel(value_hbm, after_ref, out_ref, token_ref, sem, *, start):
    copy = pltpu.make_async_copy(value_hbm.at[start : start + out_ref.shape[0]], out_ref, sem)
    copy.start()
    token_ref[...] = jnp.zeros_like(token_ref)
    copy.wait()


def fetch(value, after, start, stop):
    shape = (stop - start, *value.shape[1:])
    return call(
        functools.partial(fetch_kernel, start=start),
        "fetch",
        [HB, AN],
        [pltpu.VMEM(shape, value.dtype), TOKEN],
        [pltpu.SemaphoreType.DMA],
        moved=4 * math.prod(shape),
    )(far_memory(value), after)


def pack_kernel(*refs):
    out_ref = refs[-1]
    planes = refs[0].shape[0]
    for i in range(out_ref.shape[0] // planes):
        out_ref[i * planes : (i + 1) * planes] = refs[i][...]


def pack(parts, after):
    planes, rows, cols = parts[0].shape
    shape = pltpu.VMEM((len(parts) * planes, rows, cols), BF)
    return call(pack_kernel, "pack", [VM] * len(parts) + [AN] * len(after), [shape])(*map(resident, parts), *after)[0]


def fill_table(table_ref, parts):
    at = 0
    for part in parts:
        table_ref[at : at + part.shape[0]] = part[...]
        at += part.shape[0]
    table_ref[at] = jnp.zeros(table_ref.shape[1:], BF)


def coupling(table_ref, where_ref, row, blocks_ref):
    slots, rank = blocks_ref.shape[0], blocks_ref.shape[1]
    rows = jnp.concatenate([table_ref[where_ref[row, k]] for k in range(slots)], axis=1)
    return jnp.dot(rows, blocks_ref[...].reshape(slots * rank, rank), preferred_element_type=F32)


def late_coupling(columns, where_ref, row, blocks_ref, z, height):
    rows, blocks = [], []
    for i, column_ref in enumerate(columns):
        for step in range(3):
            if 0 <= z + step - 1 < height:
                slot = where_ref[row, 3 * i + step]
                plane = column_ref[z + step - 1]
                rows.append(jnp.where(slot >= 0, plane, jnp.zeros_like(plane)))
                blocks.append(blocks_ref[jnp.maximum(slot, 0)])
    return jnp.dot(jnp.concatenate(rows, axis=1), jnp.concatenate(blocks, axis=0), preferred_element_type=F32)


def early_lower_kernel(*refs):
    where_ref, parts, refs = refs[0], [refs[i] for i in (4, 3, 2, 1)], refs[5:]
    skel_ref, low_ref, fill_hbm, out_ref, child_ref, high_ref, table_ref, child_vmem, sems = refs
    height, planes, done = out_ref.shape[0], parts[1].shape[0], low_ref.shape[0]
    block = high_ref.shape[0] // (sems.shape[0] - 1)
    loads = []
    for i in range(sems.shape[0] - 1):
        source = fill_hbm.at[done + i * block : done + (i + 1) * block]
        loads.append(pltpu.make_async_copy(source, high_ref.at[i * block : (i + 1) * block], sems.at[i]))
        loads[-1].start()
    lane = lax.broadcasted_iota(jnp.int32, child_vmem.shape, 1)
    level = lax.broadcasted_iota(jnp.int32, child_vmem.shape, 0)
    found = jnp.zeros(child_vmem.shape, jnp.int32)
    columns = [part[at] for part in (parts[0], parts[2]) for at in (height, planes + height)]
    for i, column in enumerate(columns):
        slots = column.astype(F32)[:height].astype(jnp.int32)
        found = found + jnp.where(slots == lane, i * height + level, 0)
    child_vmem[...] = found
    copy = pltpu.make_async_copy(child_vmem, child_ref, sems.at[len(loads)])
    copy.start()
    fill_table(table_ref, parts)
    for z in range(height):
        if z >= done and (z - done) % block == 0:
            loads[(z - done) // block].wait()
        blocks_ref = low_ref.at[z] if z < done else high_ref.at[z - done]
        out_ref[z] = skel_ref[z] - coupling(table_ref, where_ref, z, blocks_ref)
    copy.wait()


def early_lower(where, parts, skel, low, fill):
    height, rhs_count, rank = skel.shape
    planes = sum(part.shape[0] for part in parts) + 1
    return call(
        early_lower_kernel,
        "early_lower",
        [SM] + [VM] * 6 + [HB],
        [
            pltpu.VMEM((height, rhs_count, rank), F32),
            pltpu.SMEM((height, rank), jnp.int32),
            pltpu.VMEM((height - low.shape[0], *fill.shape[1:]), BF),
        ],
        [
            pltpu.VMEM((planes, rhs_count, rank), BF),
            pltpu.VMEM((height, rank), jnp.int32),
            pltpu.SemaphoreType.DMA((5,)),
        ],
        moved=16 << 20,
    )(scalars(where), *map(resident, (*parts[::-1], skel, low)), far_memory(fill))


def late_lower_kernel(where_ref, odd_ref, even_ref, base_ref, low_ref, high_ref, out_ref):
    height, done = out_ref.shape[0], low_ref.shape[0]
    for z in range(height):
        blocks_ref = low_ref.at[z] if z < done else high_ref.at[z - done]
        out_ref[z] = (base_ref[z] - late_coupling((even_ref, odd_ref), where_ref, 2 * height + z, blocks_ref, z, height)).astype(BF)


def late_lower(where, columns, base, low, high):
    shape = pltpu.VMEM(base.shape, BF)
    operands = (*columns[::-1], base, low, high)
    return call(late_lower_kernel, "late_lower", [SM] + [VM] * 5, [shape])(scalars(where), *map(resident, operands))[0]


def parent_kernel(child_ref, own_ref, far_ref, rows_ref, out_ref, table_ref):
    planes = own_ref.shape[0]
    table_ref[0:planes] = own_ref[...]
    table_ref[planes : 2 * planes] = far_ref[...]
    for i in range(out_ref.shape[0] // 2):
        places = [child_ref[2 * i, s] + child_ref[2 * i + 1, s] for s in range(8)]
        stacked = jnp.concatenate([table_ref[place] for place in places], axis=1)
        for z in (2 * i, 2 * i + 1):
            out_ref[z] = jnp.dot(stacked, rows_ref[z], preferred_element_type=F32).astype(BF)


def parent(child, own, far, rows):
    height, rhs_count, rank = rows.shape[0], own.shape[1], own.shape[2]
    return call(
        parent_kernel,
        "parent",
        [SM, VM, VM, VM],
        [pltpu.VMEM((height, rhs_count, rank), BF)],
        [pltpu.VMEM((2 * own.shape[0], rhs_count, rank), BF)],
    )(scalars(child), resident(own), resident(far), resident(rows))[0]


LAST = (((1,), (1,)), ((), ()))


def half_kernel(skel_ref, transform_ref, out_ref, token_ref):
    rank = skel_ref.shape[2]
    for z in range(out_ref.shape[0]):
        out_ref[z] = lax.dot_general(skel_ref[z], transform_ref[z, :, rank:], LAST, preferred_element_type=F32)
    token_ref[...] = jnp.zeros_like(token_ref)


def half(skel, transform):
    height, rhs_count, rank = skel.shape
    shape = pltpu.VMEM((height, rhs_count, transform.shape[1]), F32)
    return call(half_kernel, "half", [VM, VM], [shape, TOKEN], moved=4 << 20)(resident(skel), resident(transform))


def early_upper_kernel(*refs):
    where_ref, parts, refs = refs[0], [refs[i] for i in (4, 3, 2, 1)], refs[5:]
    local_ref, low_ref, high_ref, out_ref, table_ref = refs
    fill_table(table_ref, parts)
    height, done = out_ref.shape[0], low_ref.shape[0]
    for z in range(height):
        blocks_ref = low_ref.at[z] if z < done else high_ref.at[z - done]
        out_ref[z] = local_ref[z].astype(F32) - coupling(table_ref, where_ref, height + z, blocks_ref)


def early_upper(where, parts, local, low, high):
    height, rhs_count, rank = parts[1].shape
    planes = sum(part.shape[0] for part in parts) + 1
    return call(
        early_upper_kernel,
        "early_upper",
        [SM] + [VM] * 7,
        [pltpu.VMEM((height, rhs_count, rank), F32)],
        [pltpu.VMEM((planes, rhs_count, rank), BF)],
        moved=16 << 20,
    )(scalars(where), *map(resident, (*parts[::-1], local, low, high)))[0]


def late_upper_kernel(where_ref, odd_ref, even_ref, base_ref, solved_ref, low_ref, high_ref, transform_ref, out_hbm, red_ref, out_ref, sems):
    height, rank, done = base_ref.shape[0], base_ref.shape[2], low_ref.shape[0]
    for z in range(height):
        blocks_ref = low_ref.at[z] if z < done else high_ref.at[z - done]
        backward = late_coupling((even_ref, odd_ref), where_ref, 2 * height + z, blocks_ref, z, height)
        red_ref[z] = (base_ref[z] - backward).astype(BF)
    copies = []
    block = height // sems.shape[0]
    for z in range(height):
        solved = lax.dot_general(red_ref[z], transform_ref[z, :, :rank], LAST, preferred_element_type=F32)
        out_ref[z] = (solved + solved_ref[z]).astype(BF)
        if (z + 1) % block == 0:
            part = slice(z + 1 - block, z + 1)
            copies.append(pltpu.make_async_copy(out_ref.at[part], out_hbm.at[part], sems.at[z // block]))
            copies[-1].start()
    for copy in copies:
        copy.wait()


def late_upper(where, columns, base, solved, low, high, transform):
    operands = (*columns[::-1], base, solved, low, high, transform)
    return call(
        late_upper_kernel,
        "late_upper",
        [SM] + [VM] * 7,
        [pltpu.HBM(solved.shape, BF)],
        [pltpu.VMEM(base.shape, BF), pltpu.VMEM(solved.shape, BF), pltpu.SemaphoreType.DMA((2,))],
    )(scalars(where), *map(resident, operands))[0]


def halo(field, before, between):
    odd = odd_swap(field, "bx")
    even = even_swap(field, "bx")
    near = pack([field, even], before)
    tokens = between(near)
    odd = pack([odd], tokens)
    for _ in range(3):
        odd = pack([odd], [])
    early = [near, odd, even_swap(near, "by"), odd_swap(near, "by")]
    return early, [even_swap(odd, "by"), odd_swap(odd, "by")]


def body(right_sides, transform, inverse, fill_lower, fill_upper, parent_rows, neighbours, counts, child_slot):
    height = right_sides.shape[2]
    skel, field, transform = first(right_sides[0, 0], transform[0, 0], inverse[0, 0], child_slot[0])
    found = []

    def between(near):
        found.extend(places(neighbours[0, 0], counts[0], (height + 1, height), fill_lower[0, 0], height // 4, near))
        return found[1:2]

    early, late = halo(field, [], between)
    where, _, low = found
    base, child, high = early_lower(where, early, skel, low, fill_lower[0, 0])
    reduced = late_lower(where, late, base, low, high)
    rows, rows_token = fetch(parent_rows[0, 0], reduced, 0, height)
    low, low_token = fetch(fill_upper[0, 0], reduced, 0, height // 2)
    pair = pack([reduced, even_swap(reduced, "bx")], [rows_token, low_token])
    skel_sol = parent(child, pair, even_swap(pair, "by"), rows)
    solved, solved_token = half(skel_sol, transform)
    high = []

    def between(near):
        value, token = fetch(fill_upper[0, 0], near, height // 2, height)
        high.append(value)
        return [token]

    early, late = halo(skel_sol, [solved_token], between)
    base = early_upper(where, early, field, low, high[0])
    solved = late_upper(where, late, base, solved, low, high[0], transform)
    return solved[None, None]


def solution(mesh):
    wide = P("bx", "by", None, None, None)
    placed = (wide, wide, wide, P("bx", "by", None, None, None, None), P("bx", "by", None, None, None, None), wide)
    placed = placed + (P("bx", "by", None, None), P("bx", "by", None), P("bx", "by", None))
    return jax.shard_map(body, mesh=mesh, in_specs=placed, out_specs=wide, check_vma=False)
```
